256 devices in a mesh: fsdp: 32 (over x_lo, z, core), ep: 8 (over x_hi, y).
Axes of the slice: x: 4 (x_hi: 2, x_lo: 2; x = x_hi * 2 + x_lo), y: 4, z: 8, core: 2. Of those that a mesh axis runs over, the one named last changes fastest.
Arguments:
- tokens: bfloat16 [1024, 6144], P('ep'), may hold values from -6 to 6
- out_grad: bfloat16 [1024, 6144], P('ep'), may hold values from -6 to 6
- router_weight: float32 [6144, 8], replicated, may hold values from -0.15625 to 0.15625
- expert_in: bfloat16 [8, 6144, 5376], P('ep', None, 'fsdp'), may hold values from -0.078125 to 0.078125
- expert_out: bfloat16 [8, 5376, 6144], P('ep', 'fsdp'), may hold values from -0.078125 to 0.078125
- choices: int32 [1024, 2], P('ep'), may hold values from 0 to 7, as said below
- slots: int32 [1024, 2], P('ep'), may hold values from -1 to 31, as said below
Outputs:
- grad_tokens: bfloat16 [1024, 6144], P('ep', 'fsdp')
- grad_in: bfloat16 [8, 6144, 5376], P('ep', None, 'fsdp')
- grad_out: bfloat16 [8, 5376, 6144], P('ep', 'fsdp')
- grad_router: float32 [6144, 8], replicated
The draws below stay inside these ranges and needn't reach their ends.
Inputs may be any that keep to these rules, and one draw needn't show every extreme that they name: `choices`: each row names two different experts. Within each aligned block of 128 rows, each slot value of 0 or more occurs at most once for each expert, and a choice is dropped only if all 32 slots of its expert are taken there; in every block some expert has all 32 slots taken.
All inputs are finite; a program needn't handle non-finite values.
Results may differ from the reference program's by a relative error of at most 0.019.
Values may be sent and summed in bfloat16 or wider, within the bound.
No kernel may reach another device: no remote copies, remote signals or barrier semaphores. Data moves between devices by JAX's collectives and lax.ppermute only.
A program may use at most 128 MiB of HBM per device.

```python
import jax
import jax.numpy as jnp
from jax import lax

D = 6144
FF = 5376
TOK_DEV = 128
EXPERTS = 8
CAP = 32
TOKENS = 1024


def route_pair(key):
    block_count = TOKENS // TOK_DEV
    hot_count = min(TOK_DEV // 2, CAP + 1)
    key_hot, key_order, key_first, key_offset, key_rank = jax.random.split(key, 5)
    hot_expert = jax.random.randint(key_hot, (block_count,), 0, EXPERTS)
    order_keys = jax.random.split(key_order, block_count)
    order = jax.vmap(lambda k: jax.random.permutation(k, TOK_DEV))(order_keys)
    is_hot = order < hot_count
    first_free = jax.random.randint(key_first, (block_count, TOK_DEV), 0, EXPERTS)
    first_pick = jnp.where(is_hot, hot_expert[:, None], first_free)
    offset = jax.random.randint(key_offset, (block_count, TOK_DEV), 1, EXPERTS)
    second_pick = (first_pick + offset) % EXPERTS
    picks = jnp.stack([first_pick, second_pick], axis=-1).reshape(block_count, 2 * TOK_DEV)
    rank_keys = jax.random.split(key_rank, block_count)
    priority = jax.vmap(lambda k: jax.random.permutation(k, 2 * TOK_DEV))(rank_keys)
    same_expert = picks[:, :, None] == picks[:, None, :]
    earlier = priority[:, None, :] < priority[:, :, None]
    ranking = jnp.sum((same_expert & earlier).astype(jnp.int32), axis=2)
    slot_vals = jnp.where(ranking < CAP, ranking, -1)
    return (picks.reshape(TOKENS, 2).astype(jnp.int32), slot_vals.reshape(TOKENS, 2).astype(jnp.int32))


def draw_choices(key, part):
    return route_pair(key)[0]


def draw_slots(key, part):
    return route_pair(key)[1]


def level_of(stream_key, dims, shards, least, high):
    def one(axis_at, shards_of):
        draws = jax.random.uniform(jax.random.fold_in(jax.random.fold_in(stream_key, 6), axis_at), (shards_of,), jnp.float32, least / len(shards), high / len(shards))
        return jnp.repeat(jnp.exp(draws), dims[axis_at] // shards_of).reshape((-1,) + (1,) * (len(dims) - axis_at - 1))

    level = one(*shards[0])
    for cut in shards[1:]:
        level = level * one(*cut)
    return level


def gaussian(stream_key, shape, spread, bound, pieces=(), kind=jnp.bfloat16):
    values = spread * jax.random.normal(stream_key, shape, jnp.float32)
    if pieces:
        values = values * level_of(stream_key, shape, pieces, -0.22, 0.18)
    return jnp.clip(values, -bound, bound).astype(kind)


def setup_inputs(seed: int = 0) -> dict:
    key_of = jax.random.split(jax.random.key(seed), 8)
    tokens = gaussian(key_of[0], (TOKENS, D), 1.0, 6.0, ((0, 8),))
    out_grad = gaussian(key_of[1], (TOKENS, D), 1.0, 6.0, ((0, 8),))
    router_weight = gaussian(key_of[2], (D, EXPERTS), (D // 4) ** -0.5, 0.15625, (), jnp.float32)
    expert_in = gaussian(key_of[3], (EXPERTS, D, FF), D ** -0.5, 0.078125, ((0, 8), (2, 32)))
    expert_out = gaussian(key_of[4], (EXPERTS, FF, D), FF ** -0.5, 0.078125, ((0, 8), (1, 32)))
    choices = draw_choices(jax.random.fold_in(key_of[7], 71), 0)
    slots = draw_slots(jax.random.fold_in(key_of[7], 71), 0)
    return {"tokens": tokens, "out_grad": out_grad, "router_weight": router_weight, "expert_in": expert_in, "expert_out": expert_out, "choices": choices, "slots": slots}


def expert_pass(packed):
    rows_x, rows_dy, rows_gate, w_in, w_out = packed
    pre_act = jnp.dot(rows_x, w_in, preferred_element_type=jnp.float32)
    back_proj = jnp.dot(rows_dy, w_out.T, preferred_element_type=jnp.float32)
    sig_act = jax.nn.sigmoid(pre_act)
    hidden = (pre_act * sig_act).astype(jnp.bfloat16)
    hid_wide = hidden.astype(jnp.float32)
    row_score = jnp.sum(hid_wide * back_proj, axis=1)
    gate_wide = rows_gate.astype(jnp.float32)[:, None]
    weighted = (hid_wide * gate_wide).astype(jnp.bfloat16)
    act_grad = (gate_wide * back_proj * sig_act * (1.0 + pre_act * (1.0 - sig_act))).astype(jnp.bfloat16)
    grad_out = jnp.dot(weighted.T, rows_dy, preferred_element_type=jnp.float32).astype(jnp.bfloat16)
    grad_in = jnp.dot(rows_x.T, act_grad, preferred_element_type=jnp.float32).astype(jnp.bfloat16)
    row_grad = jnp.dot(act_grad, w_in.T, preferred_element_type=jnp.float32)
    return grad_in, grad_out, row_grad, row_score


def reference(tokens, out_grad, router_weight, expert_in, expert_out, choices, slots):
    tok_all = tokens.shape[0]
    blocks = tok_all // TOK_DEV
    slot_rows = blocks * CAP
    tokens_wide = tokens.astype(jnp.float32)
    logits = jnp.dot(tokens_wide, router_weight, precision=lax.Precision.HIGHEST)
    chosen = jnp.take_along_axis(logits, choices, axis=1)
    first_gate = 1.0 / (1.0 + jnp.exp(chosen[:, 1] - chosen[:, 0]))
    second_gate = 1.0 / (1.0 + jnp.exp(chosen[:, 0] - chosen[:, 1]))
    gate_pair = jnp.stack([first_gate, second_gate], axis=1).astype(jnp.bfloat16)
    kept_mask = slots >= 0
    block_ids = (jnp.arange(tok_all, dtype=jnp.int32) // TOK_DEV)[:, None]
    row_index = block_ids * CAP + jnp.maximum(slots, 0)
    row_drop = jnp.where(kept_mask, row_index, slot_rows).astype(jnp.int32)
    row_safe = jnp.where(kept_mask, row_index, 0).astype(jnp.int32)
    model_width = tokens.shape[1]
    spread_x = jnp.broadcast_to(tokens[:, None, :], (tok_all, 2, model_width))
    spread_dy = jnp.broadcast_to(out_grad[:, None, :], (tok_all, 2, model_width))
    buffer_x = jnp.zeros((EXPERTS, slot_rows, model_width), jnp.bfloat16).at[choices, row_drop].set(spread_x, mode="drop")
    buffer_dy = jnp.zeros((EXPERTS, slot_rows, model_width), jnp.bfloat16).at[choices, row_drop].set(spread_dy, mode="drop")
    buffer_gate = jnp.zeros((EXPERTS, slot_rows), jnp.bfloat16).at[choices, row_drop].set(gate_pair, mode="drop")
    grad_in, grad_out, row_grads, row_scores = lax.map(expert_pass, (buffer_x, buffer_dy, buffer_gate, expert_in, expert_out))
    kept_wide = kept_mask.astype(jnp.float32)
    expert_grad = jnp.zeros((tok_all, model_width), jnp.float32)
    for which in range(2):
        picked_rows = row_grads[choices[:, which], row_safe[:, which]]
        expert_grad = expert_grad + picked_rows * kept_wide[:, which][:, None]
    taken_score = row_scores[choices, row_safe] * kept_wide
    change = first_gate * second_gate * (taken_score[:, 0] - taken_score[:, 1])
    expert_ids = jnp.arange(EXPERTS, dtype=jnp.int32)
    first_hot = (choices[:, 0:1] == expert_ids[None, :]).astype(jnp.float32)
    second_hot = (choices[:, 1:2] == expert_ids[None, :]).astype(jnp.float32)
    logit_grad = change[:, None] * (first_hot - second_hot)
    grad_tokens = (expert_grad + jnp.dot(logit_grad, router_weight.T, precision=lax.Precision.HIGHEST)).astype(jnp.bfloat16)
    grad_router = jnp.dot(tokens_wide.T, logit_grad, precision=lax.Precision.HIGHEST) / tok_all
    return grad_tokens, grad_in, grad_out, grad_router
```

```python
import jax
import jax.numpy as jnp
from jax import lax
from jax.sharding import PartitionSpec as P

F32 = jnp.float32
BF16 = jnp.bfloat16
Z = 8
EP = 8


def fsdp_pairs(move):
    pairs = []
    for lo in range(2):
        for z in range(Z):
            for core in range(2):
                a, b, c = move(lo, z, core)
                pairs.append(((lo * Z + z) * 2 + core, ((a % 2) * Z + b % Z) * 2 + c % 2))
    return pairs


TO_CORE = fsdp_pairs(lambda lo, z, core: (lo, z, core + 1))
TO_UP = fsdp_pairs(lambda lo, z, core: (lo, z + 1, core))
TO_DOWN = fsdp_pairs(lambda lo, z, core: (lo, z - 1, core))
TO_SIDE = fsdp_pairs(lambda lo, z, core: (lo + 1, z, core))
TO_FLIP = {k: fsdp_pairs(lambda lo, z, core, k=k: (lo, z ^ k, core)) for k in (1, 2, 4)}
TO_EXPERT = {r: [(e, e ^ r) for e in range(EP)] for r in range(1, EP)}


def send(array, pairs):
    return lax.ppermute(array, "fsdp", pairs)


def send_ep(array, r):
    return lax.ppermute(array, "ep", TO_EXPERT[r])


def dot(left, right, dims):
    return lax.dot_general(left, right, (dims, ((), ())), preferred_element_type=F32)


def split3(array):
    high = lax.reduce_precision(array, 8, 7)
    rest = array - high
    mid = lax.reduce_precision(rest, 8, 7)
    low = rest - mid
    return high.astype(BF16), mid.astype(BF16), low.astype(BF16)


def columns(array, start, size):
    return lax.dynamic_slice_in_dim(array, start, size, 1)


def per_device(tokens, out_grad, router_weight, expert_in, expert_out, choices, slots):
    tok_rows, width = tokens.shape
    experts = router_weight.shape[1]
    capacity = max(2, 2 * tok_rows // experts)
    half = capacity // 2
    rows = experts * half
    fsdp_index = lax.axis_index("fsdp")
    me = lax.axis_index("ep")
    core = fsdp_index % 2
    z = (fsdp_index // 2) % Z
    lo = fsdp_index // (2 * Z)
    shard = width // Z
    seg = width // (2 * Z)
    own_cols = width // (4 * Z)

    w_in = expert_in[0].T
    w_out = expert_out[0]

    key = ((slots // half) ^ core) * rows + (choices ^ me) * half + slots % half
    key = jnp.where(slots >= 0, key, -1)
    places = key[:, :, None] == jnp.arange(2 * rows, dtype=jnp.int32)
    spread = (places[:, 0] | places[:, 1])[:, :rows].astype(BF16)

    picked = jnp.concatenate(
        [columns(out_grad, ((z + k) % Z) * shard, shard) for k in (5, 0, 3)], axis=1
    )
    send_dy = dot(spread, picked, ((0,), (0,))).astype(BF16)
    got_dy = [send_dy[:half]] + [
        send_ep(send_dy[r * half : (r + 1) * half], r) for r in range(1, experts)
    ]
    dy3 = jnp.concatenate(got_dy, axis=0)

    parts = split3(router_weight)
    logits = dot(tokens, jnp.concatenate(parts, axis=1), ((1,), (0,)))
    logits = (logits[:, :experts] + logits[:, experts : 2 * experts]) + logits[:, 2 * experts :]
    chosen_hot = (choices[:, :, None] == jnp.arange(experts, dtype=jnp.int32)).astype(F32)
    chosen = jnp.sum(chosen_hot * logits[:, None, :], axis=2)
    first_gate = 1.0 / (1.0 + jnp.exp(chosen[:, 1] - chosen[:, 0]))
    second_gate = 1.0 / (1.0 + jnp.exp(chosen[:, 0] - chosen[:, 1]))
    gate_pair = jnp.stack([first_gate, second_gate], axis=1).astype(BF16).astype(F32)
    near_hot = (choices ^ me)[:, :, None] == jnp.arange(128, dtype=jnp.int32)
    gate_cols = jnp.sum(jnp.where(near_hot, gate_pair[:, :, None], 0.0), axis=1).astype(BF16)

    send_x = dot(
        spread, jnp.concatenate([tokens, gate_cols], axis=1), ((0,), (0,))
    ).astype(BF16)
    got_x = [send_x[:half]] + [
        send_ep(send_x[r * half : (r + 1) * half], r) for r in range(1, experts)
    ]
    x_mine = jnp.concatenate(got_x, axis=0)

    cut = seg
    from_up = send(dy3[:, : 5 * cut], TO_DOWN)
    from_down = send(dy3[:, cut:], TO_UP)
    dy_mine = jnp.concatenate(
        [
            dy3[:, 2 * cut : 4 * cut],
            from_up[:, 2 * cut : 4 * cut],
            from_down[:, 3 * cut :],
            dy3[:, 4 * cut :],
            from_up[:, 4 * cut :],
            from_down[:, :cut],
            dy3[:, : 2 * cut],
            from_up[:, : 2 * cut],
            from_down[:, cut : 3 * cut],
        ],
        axis=1,
    )
    x_other = send(x_mine, TO_CORE)
    dy_other = send(dy_mine, TO_CORE)
    rows_x = jnp.concatenate([x_mine, x_other], axis=0)
    rows_dy = jnp.concatenate([dy_mine, dy_other], axis=0)
    w_out_near = jnp.concatenate(
        [columns(w_out, ((z + k) % Z) * shard, shard) for k in range(Z)], axis=1
    )
    block = (jnp.arange(2 * rows, dtype=jnp.int32) % rows) // half
    gate = jnp.sum(
        jnp.where(
            block[:, None] == jnp.arange(128, dtype=jnp.int32)[None, :],
            rows_x[:, width:].astype(F32),
            0.0,
        ),
        axis=1,
        keepdims=True,
    )
    rows_x = rows_x[:, :width]

    pre = dot(rows_x, w_in, ((1,), (1,)))
    back = dot(rows_dy, w_out_near, ((1,), (1,)))
    sig = jax.nn.sigmoid(pre)
    hidden = (pre * sig).astype(BF16)
    hid_wide = hidden.astype(F32)
    score = jnp.sum(hid_wide * back, axis=1)
    weighted = (hid_wide * gate).astype(BF16)
    act_grad = (gate * back * sig * (1.0 + pre * (1.0 - sig))).astype(BF16)

    part_other = dot(act_grad[rows:], w_in, ((1,), (0,))).astype(BF16)
    from_core = send(part_other, TO_CORE)
    part = (dot(act_grad[:rows], w_in, ((1,), (0,))) + from_core.astype(F32)).astype(BF16)

    def piece(k):
        at = (z + k) % Z
        return jnp.concatenate(
            [columns(part, ((lo ^ d) * Z + at) * seg, seg) for d in range(2)], axis=1
        ).astype(F32)

    up = send(piece(4).astype(BF16), TO_UP)
    down = send(piece(5).astype(BF16), TO_DOWN)
    up = send((up.astype(F32) + piece(3)).astype(BF16), TO_UP)
    down = send((down.astype(F32) + piece(6)).astype(BF16), TO_DOWN)
    up = send((up.astype(F32) + piece(2)).astype(BF16), TO_UP)
    down = send((down.astype(F32) + piece(7)).astype(BF16), TO_DOWN)
    up = send((up.astype(F32) + piece(1)).astype(BF16), TO_UP)
    total = up.astype(F32) + down.astype(F32) + piece(0)
    side = send(total[:, seg:].astype(BF16), TO_SIDE)
    own = (total[:, :seg] + side.astype(F32)).astype(BF16)
    returned = jnp.concatenate(
        [own[:half]]
        + [send_ep(own[r * half : (r + 1) * half], r) for r in range(1, experts)],
        axis=0,
    )
    merged = dot(spread, returned, ((1,), (0,)))
    low_cols, high_cols = merged[:, :own_cols], merged[:, own_cols:]
    keep = jnp.where(core == 0, low_cols, high_cols)
    give = jnp.where(core == 0, high_cols, low_cols)
    expert_grad = keep + send(give.astype(BF16), TO_CORE).astype(F32)

    pair = score.reshape(2, rows)
    pair = pair + send(pair, TO_CORE)[::-1]
    pair = pair + send(pair, TO_FLIP[1])
    pair = pair + send(pair, TO_FLIP[2])
    pair = pair + send(pair, TO_FLIP[4])
    pair = pair + send(pair, TO_SIDE)
    back_scores = jnp.concatenate(
        [pair[:, :half]]
        + [send_ep(pair, r)[:, r * half : (r + 1) * half] for r in range(1, experts)],
        axis=1,
    ).reshape(2 * rows)
    taken = jnp.sum(jnp.where(places, back_scores[None, None, :], 0.0), axis=2)
    change = first_gate * second_gate * (taken[:, 0] - taken[:, 1])
    logit_grad = change[:, None] * (chosen_hot[:, 0, :] - chosen_hot[:, 1, :])

    router_part = dot(jnp.concatenate(split3(logit_grad), axis=1), tokens, ((0,), (0,)))
    router_part = (router_part[:experts] + router_part[experts : 2 * experts]) + router_part[
        2 * experts :
    ]
    chunk = width // EP
    mine = columns(router_part, me * chunk, chunk)
    for r in range(1, EP):
        mine = mine + send_ep(columns(router_part, (me ^ r) * chunk, chunk), r)
    mine = mine / (tok_rows * EP)
    gathered = [mine] + [send_ep(mine, r) for r in range(1, EP)]
    grad_router = jnp.zeros((experts, width), F32)
    for r in range(EP):
        grad_router = lax.dynamic_update_slice_in_dim(
            grad_router, gathered[r], (me ^ r) * chunk, 1
        )

    grad_out_near = dot(weighted, rows_dy, ((0,), (0,))).astype(BF16)
    grad_out = jnp.concatenate(
        [columns(grad_out_near, ((k - z) % Z) * shard, shard) for k in range(Z)], axis=1
    )
    grad_in = dot(act_grad, rows_x, ((0,), (0,))).astype(BF16)

    router_rows = lax.dynamic_slice_in_dim(router_weight, fsdp_index * own_cols, own_cols, 0)
    grad_tokens = (
        expert_grad + jnp.dot(logit_grad, router_rows.T, precision=lax.Precision.HIGHEST)
    ).astype(BF16)
    return grad_tokens, grad_in.T[None], grad_out[None], grad_router.T


def solution(mesh):
    placed = (
        P("ep", None),
        P("ep", None),
        P(),
        P("ep", None, "fsdp"),
        P("ep", "fsdp", None),
        P("ep", None),
        P("ep", None),
    )
    return jax.shard_map(
        per_device,
        mesh=mesh,
        in_specs=placed,
        out_specs=(P("ep", "fsdp"), P("ep", None, "fsdp"), P("ep", "fsdp", None), P()),
        check_vma=False,
    )
```

```python
import jax
import jax.numpy as jnp
from jax import lax
from jax.sharding import PartitionSpec as P

F32 = jnp.float32
BF16 = jnp.bfloat16
Z = 8
EP = 8


def fsdp_pairs(move):
    pairs = []
    for lo in range(2):
        for z in range(Z):
            for core in range(2):
                a, b, c = move(lo, z, core)
                pairs.append(((lo * Z + z) * 2 + core, ((a % 2) * Z + b % Z) * 2 + c % 2))
    return pairs


TO_CORE = fsdp_pairs(lambda lo, z, core: (lo, z, core + 1))
TO_UP = fsdp_pairs(lambda lo, z, core: (lo, z + 1, core))
TO_DOWN = fsdp_pairs(lambda lo, z, core: (lo, z - 1, core))
TO_SIDE = fsdp_pairs(lambda lo, z, core: (lo + 1, z, core))


def send(array, pairs):
    return lax.ppermute(array, "fsdp", pairs)


def dot(left, right, dims):
    return lax.dot_general(left, right, (dims, ((), ())), preferred_element_type=F32)


def split3(array):
    high = lax.reduce_precision(array, 8, 7)
    rest = array - high
    mid = lax.reduce_precision(rest, 8, 7)
    low = rest - mid
    return high.astype(BF16), mid.astype(BF16), low.astype(BF16)


def columns(array, start, size):
    return lax.dynamic_slice_in_dim(array, start, size, 1)


def per_device(tokens, out_grad, router_weight, expert_in, expert_out, choices, slots):
    tok_rows, width = tokens.shape
    experts = router_weight.shape[1]
    capacity = max(2, 2 * tok_rows // experts)
    half = capacity // 2
    rows = experts * half
    fsdp_index = lax.axis_index("fsdp")
    me = lax.axis_index("ep")
    core = fsdp_index % 2
    z = (fsdp_index // 2) % Z
    lo = fsdp_index // (2 * Z)
    seg = width // (2 * Z)
    own_cols = width // (4 * Z)

    w_in = expert_in[0].T
    w_out = expert_out[0]

    parts = split3(router_weight)
    logits = dot(tokens, jnp.concatenate(parts, axis=1), ((1,), (0,)))
    logits = (logits[:, :experts] + logits[:, experts : 2 * experts]) + logits[:, 2 * experts :]
    chosen_hot = (choices[:, :, None] == jnp.arange(experts, dtype=jnp.int32)).astype(F32)
    chosen = jnp.sum(chosen_hot * logits[:, None, :], axis=2)
    first_gate = 1.0 / (1.0 + jnp.exp(chosen[:, 1] - chosen[:, 0]))
    second_gate = 1.0 / (1.0 + jnp.exp(chosen[:, 0] - chosen[:, 1]))
    gate_pair = jnp.stack([first_gate, second_gate], axis=1).astype(BF16).astype(F32)
    expert_hot = choices[:, :, None] == jnp.arange(128, dtype=jnp.int32)
    gate_cols = jnp.sum(jnp.where(expert_hot, gate_pair[:, :, None], 0.0), axis=1).astype(BF16)

    key_abs = jnp.where((slots // half == core) & (slots >= 0), choices * half + slots % half, -1)
    places_abs = key_abs[:, :, None] == jnp.arange(rows, dtype=jnp.int32)
    spread_abs = (places_abs[:, 0] | places_abs[:, 1]).astype(BF16)
    packed = jnp.concatenate([out_grad, tokens, gate_cols], axis=1)
    send_rows = dot(spread_abs, packed, ((0,), (0,))).astype(BF16)
    mine_rows = lax.all_to_all(
        send_rows.reshape(experts, half, 2 * width + 128), "ep", 0, 0, tiled=True
    ).reshape(rows, 2 * width + 128)
    other_rows = send(mine_rows, TO_CORE)
    both = jnp.concatenate([mine_rows, other_rows], axis=0)
    rows_dy = both[:, :width]
    rows_x = both[:, width : 2 * width]
    gate = jnp.sum(
        jnp.where(
            jnp.arange(128, dtype=jnp.int32)[None, :] == me,
            both[:, 2 * width :].astype(F32),
            0.0,
        ),
        axis=1,
        keepdims=True,
    )

    pre = dot(rows_x, w_in, ((1,), (1,)))
    back = dot(rows_dy, w_out, ((1,), (1,)))
    sig = jax.nn.sigmoid(pre)
    hidden = (pre * sig).astype(BF16)
    hid_wide = hidden.astype(F32)
    score = jnp.sum(hid_wide * back, axis=1)
    weighted = (hid_wide * gate).astype(BF16)
    act_grad = (gate * back * sig * (1.0 + pre * (1.0 - sig))).astype(BF16)

    part_other = dot(act_grad[rows:], w_in, ((1,), (0,))).astype(BF16)
    from_core = send(part_other, TO_CORE)
    part = (dot(act_grad[:rows], w_in, ((1,), (0,))) + from_core.astype(F32)).astype(BF16)

    def piece(k):
        at = (z + k) % Z
        return jnp.concatenate(
            [columns(part, ((lo ^ d) * Z + at) * seg, seg) for d in range(2)], axis=1
        ).astype(F32)

    up, down = piece(4), piece(5)
    for step in range(3):
        up, down = lax.optimization_barrier((up.astype(BF16), down.astype(BF16)))
        up, down = send(up, TO_UP), send(down, TO_DOWN)
        up = up.astype(F32) + piece(3 - step)
        down = down.astype(F32) + piece((6 + step) % Z)
    total = send(up.astype(BF16), TO_UP).astype(F32) + down
    side = send(total[:, seg:].astype(BF16), TO_SIDE)
    own = (total[:, :seg] + side.astype(F32)).astype(BF16)
    returned = lax.all_to_all(own.reshape(experts, half, seg), "ep", 0, 0, tiled=True).reshape(
        rows, seg
    )
    merged = dot(spread_abs, returned, ((1,), (0,)))
    low_cols, high_cols = merged[:, :own_cols], merged[:, own_cols:]
    keep = jnp.where(core == 0, low_cols, high_cols)
    give = jnp.where(core == 0, high_cols, low_cols)
    expert_grad = keep + send(give.astype(BF16), TO_CORE).astype(F32)

    pair = score.reshape(2, rows)
    pair = jnp.where(core == 0, pair, pair[::-1]).reshape(2, experts, half)
    blocks = jnp.transpose(pair, (1, 0, 2)).reshape(experts, 1, capacity)
    fsdp_size = lax.axis_size("fsdp")
    parts = lax.all_to_all(
        jnp.broadcast_to(blocks[None], (fsdp_size,) + blocks.shape).reshape(-1, 1, capacity),
        ("fsdp", "ep"),
        0,
        0,
        tiled=True,
    )
    all_scores = jnp.sum(parts.reshape(fsdp_size, experts, capacity), axis=0).reshape(-1)
    slot_key = jnp.where(slots >= 0, choices * capacity + slots, -1)
    slot_hot = slot_key[:, :, None] == jnp.arange(experts * capacity, dtype=jnp.int32)
    taken = jnp.sum(jnp.where(slot_hot, all_scores[None, None, :], 0.0), axis=2)
    change = first_gate * second_gate * (taken[:, 0] - taken[:, 1])
    logit_grad = change[:, None] * (chosen_hot[:, 0, :] - chosen_hot[:, 1, :])

    router_part = dot(jnp.concatenate(split3(logit_grad), axis=1), tokens, ((0,), (0,)))
    router_part = (router_part[:experts] + router_part[experts : 2 * experts]) + router_part[
        2 * experts :
    ]
    chunk = width // EP
    chunks = jnp.transpose(router_part.reshape(experts, EP, chunk), (1, 0, 2))
    mine = jnp.sum(lax.all_to_all(chunks, "ep", 0, 0, tiled=True), axis=0) / (tok_rows * EP)
    gathered = lax.all_to_all(
        jnp.broadcast_to(mine[None], (EP, experts, chunk)), "ep", 0, 0, tiled=True
    )
    grad_router = jnp.transpose(gathered, (1, 0, 2)).reshape(experts, width)

    grad_out = dot(weighted, rows_dy, ((0,), (0,))).astype(BF16)
    grad_in = dot(act_grad, rows_x, ((0,), (0,))).astype(BF16)

    router_rows = lax.dynamic_slice_in_dim(router_weight, fsdp_index * own_cols, own_cols, 0)
    grad_tokens = (
        expert_grad + jnp.dot(logit_grad, router_rows.T, precision=lax.Precision.HIGHEST)
    ).astype(BF16)
    return grad_tokens, grad_in.T[None], grad_out[None], grad_router.T


def solution(mesh):
    placed = (
        P("ep", None),
        P("ep", None),
        P(),
        P("ep", None, "fsdp"),
        P("ep", "fsdp", None),
        P("ep", None),
        P("ep", None),
    )
    return jax.shard_map(
        per_device,
        mesh=mesh,
        in_specs=placed,
        out_specs=(P("ep", "fsdp"), P("ep", None, "fsdp"), P("ep", "fsdp", None), P()),
        check_vma=False,
    )
```

```python
import jax
import jax.numpy as jnp
from jax import lax
from jax.sharding import PartitionSpec as P

F32 = jnp.float32
BF16 = jnp.bfloat16
Z = 8
EP = 8


def fsdp_pairs(move):
    pairs = []
    for lo in range(2):
        for z in range(Z):
            for core in range(2):
                a, b, c = move(lo, z, core)
                pairs.append(((lo * Z + z) * 2 + core, ((a % 2) * Z + b % Z) * 2 + c % 2))
    return pairs


TO_CORE = fsdp_pairs(lambda lo, z, core: (lo, z, core + 1))
TO_UP = fsdp_pairs(lambda lo, z, core: (lo, z + 1, core))
TO_DOWN = fsdp_pairs(lambda lo, z, core: (lo, z - 1, core))
TO_SIDE = fsdp_pairs(lambda lo, z, core: (lo + 1, z, core))


def send(array, pairs):
    return lax.ppermute(array, "fsdp", pairs)


def dot(left, right, dims):
    return lax.dot_general(left, right, (dims, ((), ())), preferred_element_type=F32)


def split3(array):
    high = lax.reduce_precision(array, 8, 7)
    rest = array - high
    mid = lax.reduce_precision(rest, 8, 7)
    low = rest - mid
    return high.astype(BF16), mid.astype(BF16), low.astype(BF16)


def columns(array, start, size):
    return lax.dynamic_slice_in_dim(array, start, size, 1)


def per_device(tokens, out_grad, router_weight, expert_in, expert_out, choices, slots):
    tok_rows, width = tokens.shape
    experts = router_weight.shape[1]
    capacity = max(2, 2 * tok_rows // experts)
    half = capacity // 2
    rows = experts * half
    fsdp_index = lax.axis_index("fsdp")
    me = lax.axis_index("ep")
    core = fsdp_index % 2
    z = (fsdp_index // 2) % Z
    lo = fsdp_index // (2 * Z)
    seg = width // (2 * Z)
    own_cols = width // (4 * Z)

    w_in = expert_in[0].T
    w_out = expert_out[0]

    router_parts = jnp.concatenate(split3(router_weight), axis=1)
    logits = dot(tokens, router_parts, ((1,), (0,)))
    logits = (logits[:, :experts] + logits[:, experts : 2 * experts]) + logits[:, 2 * experts :]
    chosen_hot = (choices[:, :, None] == jnp.arange(experts, dtype=jnp.int32)).astype(F32)
    chosen = jnp.sum(chosen_hot * logits[:, None, :], axis=2)
    first_gate = 1.0 / (1.0 + jnp.exp(chosen[:, 1] - chosen[:, 0]))
    second_gate = 1.0 / (1.0 + jnp.exp(chosen[:, 0] - chosen[:, 1]))

    key_abs = jnp.where((slots // half == core) & (slots >= 0), choices * half + slots % half, -1)
    places_abs = key_abs[:, :, None] == jnp.arange(rows, dtype=jnp.int32)
    spread_abs = (places_abs[:, 0] | places_abs[:, 1]).astype(BF16)
    both_choices = jnp.broadcast_to(
        jnp.sum(choices, axis=1, keepdims=True).astype(BF16), (tok_rows, 128)
    )
    packed = jnp.concatenate([out_grad, tokens, both_choices], axis=1)
    send_rows = dot(spread_abs, packed, ((0,), (0,))).astype(BF16)
    mine_rows = lax.all_to_all(
        send_rows.reshape(experts, half, 2 * width + 128), "ep", 0, 0, tiled=True
    ).reshape(rows, 2 * width + 128)
    other_rows = send(mine_rows, TO_CORE)
    w_ext = jnp.concatenate([w_in, router_parts.T], axis=0)
    hidden_count = w_in.shape[0]

    def act(part_rows):
        ext = dot(part_rows[:, width : 2 * width], w_ext, ((1,), (1,)))
        back = dot(part_rows[:, :width], w_out, ((1,), (1,)))
        pre = ext[:, :hidden_count]
        row_logits = ext[:, hidden_count : hidden_count + experts] + (
            ext[:, hidden_count + experts : hidden_count + 2 * experts]
            + ext[:, hidden_count + 2 * experts :]
        )
        second = part_rows[:, 2 * width : 2 * width + 1].astype(jnp.int32) - me
        ids = jnp.arange(experts, dtype=jnp.int32)[None, :]
        gap = jnp.sum(
            jnp.where(ids == second, row_logits, 0.0) - jnp.where(ids == me, row_logits, 0.0),
            axis=1,
            keepdims=True,
        )
        gate_wide = 1.0 / (1.0 + jnp.exp(gap))
        slope = gate_wide * (1.0 / (1.0 + jnp.exp(-gap)))
        gate = gate_wide.astype(BF16).astype(F32)
        sig = jax.nn.sigmoid(pre)
        hidden = (pre * sig).astype(BF16)
        hid_wide = hidden.astype(F32)
        score = jnp.sum(hid_wide * back, axis=1, keepdims=True)
        weighted = (hid_wide * gate).astype(BF16)
        act_grad = (gate * back * sig * (1.0 + pre * (1.0 - sig))).astype(BF16)
        slopes = slope * ((ids == me).astype(F32) - (ids == second).astype(F32))
        return score, weighted, act_grad, slopes

    score_mine, weighted_mine, act_mine, slopes_mine = act(mine_rows)
    score_other, weighted_other, act_other, _ = act(other_rows)

    def weights(k):
        at = (z + k) % Z
        return [columns(w_in, ((lo ^ d) * Z + at) * seg, seg) for d in range(2)]

    orders = [(4, 5), (3, 6), (2, 7), (1, 0)]
    near = [jnp.concatenate(weights(a) + weights(b), axis=1) for a, b in orders]

    def pack(grads, score):
        high = lax.reduce_precision(score, 8, 7)
        lane = lax.broadcasted_iota(jnp.int32, (rows, 128), 1)
        block = jnp.where(lane == 0, high, jnp.where(lane == 1, score - high, 0.0))
        return jnp.concatenate([grads.astype(BF16), block.astype(BF16)], axis=1)

    def unpack(packed):
        wide = packed.astype(F32)
        return wide[:, :-128], jnp.sum(wide[:, -128:], axis=1, keepdims=True)

    first_other = dot(act_other, near[0], ((1,), (0,)))
    got, got_score = unpack(send(pack(first_other, score_other), TO_CORE))
    score = score_mine + got_score
    part = dot(act_mine, near[0], ((1,), (0,))) + got
    up, down = part[:, : 2 * seg], part[:, 2 * seg :]
    up_score = down_score = score
    for step in range(3):
        going_up, going_down = lax.optimization_barrier(
            (pack(up, up_score), pack(down, down_score))
        )
        up, up_score = unpack(send(going_up, TO_UP))
        down, down_score = unpack(send(going_down, TO_DOWN))
        other = dot(act_other, near[step + 1], ((1,), (0,))).astype(BF16)
        got = send(other, TO_CORE)
        part = dot(act_mine, near[step + 1], ((1,), (0,))) + got.astype(F32)
        up, up_score = up + part[:, : 2 * seg], up_score + score
        down, down_score = down + part[:, 2 * seg :], down_score + score
    last, last_score = unpack(send(pack(up, up_score), TO_UP))
    total, total_score = last + down, last_score + down_score
    side, side_score = unpack(send(pack(total[:, seg:], total_score), TO_SIDE))
    own, own_score = total[:, :seg] + side, total_score + side_score

    router_part = dot(
        jnp.concatenate(split3(slopes_mine * own_score), axis=1),
        mine_rows[:, width : 2 * width],
        ((0,), (0,)),
    )
    router_part = (router_part[:experts] + router_part[experts : 2 * experts]) + router_part[
        2 * experts :
    ]
    chunk = width // EP

    def two(array):
        high = lax.reduce_precision(array, 8, 7)
        return jnp.stack([high, array - high]).astype(BF16)

    chunks = jnp.transpose(two(router_part).reshape(2, experts, EP, chunk), (2, 0, 1, 3))

    home = lax.all_to_all(
        jnp.concatenate(
            [
                pack(own, own_score).reshape(experts, half, seg + 128),
                jnp.concatenate(
                    [
                        chunks.reshape(EP, -1, seg),
                        jnp.zeros((EP, 2 * experts * chunk // seg, 128), BF16),
                    ],
                    axis=2,
                ),
            ],
            axis=1,
        ),
        "ep",
        0,
        0,
        tiled=True,
    )
    returned, back_scores = unpack(home[:, :half].reshape(rows, seg + 128))
    router_mine = jnp.sum(
        home[:, half:, :seg].reshape(EP, 2, experts, chunk).astype(F32), axis=(0, 1)
    ) / (tok_rows * EP)
    merged = dot(spread_abs, returned, ((1,), (0,)))
    taken = jnp.sum(
        jnp.where(places_abs, back_scores.reshape(1, 1, rows), 0.0), axis=2
    )
    low_cols, high_cols = merged[:, :own_cols], merged[:, own_cols:]
    keep = jnp.where(core == 0, low_cols, high_cols)
    give = jnp.where(core == 0, high_cols, low_cols)
    expert_grad = keep + send(give.astype(BF16), TO_CORE).astype(F32)
    small = jnp.concatenate([router_mine, jnp.pad(taken.T, ((0, 6), (0, 0)))], axis=1)
    small = small + send(small, TO_CORE)
    router_mine, taken = small[:, :chunk], small[:2, chunk:].T
    change = first_gate * second_gate * (taken[:, 0] - taken[:, 1])
    logit_grad = change[:, None] * (chosen_hot[:, 0, :] - chosen_hot[:, 1, :])
    gathered = lax.all_to_all(
        jnp.broadcast_to(router_mine[None], (EP, experts, chunk)), "ep", 0, 0, tiled=True
    )
    grad_router = jnp.transpose(gathered, (1, 0, 2)).reshape(experts, width)

    both = jnp.concatenate([mine_rows, other_rows], axis=0)
    weighted = jnp.concatenate([weighted_mine, weighted_other], axis=0)
    act_grad = jnp.concatenate([act_mine, act_other], axis=0)
    grad_out = dot(weighted, both[:, :width], ((0,), (0,))).astype(BF16)
    grad_in = dot(act_grad, both[:, width : 2 * width], ((0,), (0,))).astype(BF16)

    router_rows = lax.dynamic_slice_in_dim(router_weight, fsdp_index * own_cols, own_cols, 0)
    grad_tokens = (
        expert_grad + jnp.dot(logit_grad, router_rows.T, precision=lax.Precision.HIGHEST)
    ).astype(BF16)
    return grad_tokens, grad_in.T[None], grad_out[None], grad_router.T


def solution(mesh):
    placed = (
        P("ep", None),
        P("ep", None),
        P(),
        P("ep", None, "fsdp"),
        P("ep", "fsdp", None),
        P("ep", None),
        P("ep", None),
    )
    return jax.shard_map(
        per_device,
        mesh=mesh,
        in_specs=placed,
        out_specs=(P("ep", "fsdp"), P("ep", None, "fsdp"), P("ep", "fsdp", None), P()),
        check_vma=False,
    )
```

```python
import jax
import jax.numpy as jnp
from jax import lax
from jax.sharding import PartitionSpec as P

F32 = jnp.float32
BF16 = jnp.bfloat16
Z = 8
EP = 8


def fsdp_pairs(move):
    pairs = []
    for lo in range(2):
        for z in range(Z):
            for core in range(2):
                a, b, c = move(lo, z, core)
                pairs.append(((lo * Z + z) * 2 + core, ((a % 2) * Z + b % Z) * 2 + c % 2))
    return pairs


TO_CORE = fsdp_pairs(lambda lo, z, core: (lo, z, core + 1))
TO_UP = fsdp_pairs(lambda lo, z, core: (lo, z + 1, core))
TO_DOWN = fsdp_pairs(lambda lo, z, core: (lo, z - 1, core))
TO_SIDE = fsdp_pairs(lambda lo, z, core: (lo + 1, z, core))

TO_CROSS = fsdp_pairs(lambda lo, z, core: (lo + 1, z, core + 1))


def send(array, pairs):
    return lax.ppermute(array, "fsdp", pairs)


def dot(left, right, dims):
    return lax.dot_general(left, right, (dims, ((), ())), preferred_element_type=F32)


def split3(array):
    high = lax.reduce_precision(array, 8, 7)
    rest = array - high
    mid = lax.reduce_precision(rest, 8, 7)
    low = rest - mid
    return high.astype(BF16), mid.astype(BF16), low.astype(BF16)


def columns(array, start, size):
    return lax.dynamic_slice_in_dim(array, start, size, 1)


def per_device(tokens, out_grad, router_weight, expert_in, expert_out, choices, slots):
    tok_rows, width = tokens.shape
    experts = router_weight.shape[1]
    capacity = max(2, 2 * tok_rows // experts)
    half = capacity // 2
    rows = experts * half
    fsdp_index = lax.axis_index("fsdp")
    me = lax.axis_index("ep")
    core = fsdp_index % 2
    z = (fsdp_index // 2) % Z
    lo = fsdp_index // (2 * Z)
    seg = width // (2 * Z)
    own_cols = width // (4 * Z)

    w_in = expert_in[0].T
    w_out = expert_out[0]

    key_abs = jnp.where((slots // half == core) & (slots >= 0), choices * half + slots % half, -1)
    places_abs = key_abs[:, :, None] == jnp.arange(rows, dtype=jnp.int32)
    spread_abs = (places_abs[:, 0] | places_abs[:, 1]).astype(BF16)
    both_choices = jnp.broadcast_to(
        jnp.sum(choices, axis=1, keepdims=True).astype(BF16), (tok_rows, 128)
    )
    packed = jnp.concatenate([out_grad, tokens, both_choices], axis=1)
    send_rows = dot(spread_abs, packed, ((0,), (0,))).astype(BF16)
    send_rows, w_in, router_weight = lax.optimization_barrier((send_rows, w_in, router_weight))
    mine_rows = lax.all_to_all(
        send_rows.reshape(experts, half, 2 * width + 128), "ep", 0, 0, tiled=True
    ).reshape(rows, 2 * width + 128)
    router_parts = jnp.concatenate(split3(router_weight), axis=1)
    logits = dot(tokens, router_parts, ((1,), (0,)))
    logits = (logits[:, :experts] + logits[:, experts : 2 * experts]) + logits[:, 2 * experts :]
    chosen_hot = (choices[:, :, None] == jnp.arange(experts, dtype=jnp.int32)).astype(F32)
    chosen = jnp.sum(chosen_hot * logits[:, None, :], axis=2)
    first_gate = 1.0 / (1.0 + jnp.exp(chosen[:, 1] - chosen[:, 0]))
    second_gate = 1.0 / (1.0 + jnp.exp(chosen[:, 0] - chosen[:, 1]))

    w_ext = jnp.concatenate([w_in, router_parts.T], axis=0)

    def weights(k):
        at = (z + k) % Z
        return [columns(w_in, ((lo ^ d) * Z + at) * seg, seg) for d in range(2)]

    orders = [(4, 5), (3, 6), (2, 7), (1, 0)]
    near = [jnp.concatenate(weights(a) + weights(b), axis=1) for a, b in orders]

    mine_rows, w_ext, near, first_gate, second_gate, chosen_hot = lax.optimization_barrier(
        (mine_rows, w_ext, near, first_gate, second_gate, chosen_hot)
    )
    other_rows = send(mine_rows, TO_CORE)
    hidden_count = w_in.shape[0]

    def act(part_rows):
        ext = dot(part_rows[:, width : 2 * width], w_ext, ((1,), (1,)))
        back = dot(part_rows[:, :width], w_out, ((1,), (1,)))
        pre = ext[:, :hidden_count]
        row_logits = ext[:, hidden_count : hidden_count + experts] + (
            ext[:, hidden_count + experts : hidden_count + 2 * experts]
            + ext[:, hidden_count + 2 * experts :]
        )
        second = part_rows[:, 2 * width : 2 * width + 1].astype(jnp.int32) - me
        ids = jnp.arange(experts, dtype=jnp.int32)[None, :]
        gap = jnp.sum(
            jnp.where(ids == second, row_logits, 0.0) - jnp.where(ids == me, row_logits, 0.0),
            axis=1,
            keepdims=True,
        )
        gate_wide = 1.0 / (1.0 + jnp.exp(gap))
        slope = gate_wide * (1.0 / (1.0 + jnp.exp(-gap)))
        gate = gate_wide.astype(BF16).astype(F32)
        sig = jax.nn.sigmoid(pre)
        hidden = (pre * sig).astype(BF16)
        hid_wide = hidden.astype(F32)
        score = jnp.sum(hid_wide * back, axis=1)[None]
        weighted = (hid_wide * gate).astype(BF16)
        act_grad = (gate * back * sig * (1.0 + pre * (1.0 - sig))).astype(BF16)
        slopes = slope * ((ids == me).astype(F32) - (ids == second).astype(F32))
        return score, weighted, act_grad, slopes

    done_mine = act(mine_rows)
    other_rows, done_mine = lax.optimization_barrier((other_rows, done_mine))
    score_mine, weighted_mine, act_mine, slopes_mine = done_mine
    score_other, weighted_other, act_other, slopes_other = act(other_rows)

    def pack(grads, score):
        high = lax.reduce_precision(score, 8, 7)
        block = jnp.concatenate([high, score - high], axis=0)
        block = jnp.pad(block, ((0, 6), (0, grads.shape[1] - rows)))
        return jnp.concatenate([grads, block], axis=0).astype(BF16)

    def unpack(packed):
        wide = packed.astype(F32)
        return wide[:rows], jnp.sum(wide[rows:, :rows], axis=0, keepdims=True)

    first_other = dot(act_other, near[0], ((1,), (0,)))
    got, got_score = unpack(send(pack(first_other, score_other), TO_CORE))
    score = score_mine + got_score
    part = dot(act_mine, near[0], ((1,), (0,))) + got
    up, down = part[:, : 2 * seg], part[:, 2 * seg :]
    up_score = down_score = score
    for step in range(3):
        going_up, going_down = lax.optimization_barrier(
            (pack(up, up_score), pack(down, down_score))
        )
        up, up_score = unpack(send(going_up, TO_UP))
        down, down_score = unpack(send(going_down, TO_DOWN))
        other = dot(act_other, near[step + 1], ((1,), (0,))).astype(BF16)
        got = send(other, TO_CORE)
        part = dot(act_mine, near[step + 1], ((1,), (0,))) + got.astype(F32)
        up, up_score = up + part[:, : 2 * seg], up_score + score
        down, down_score = down + part[:, 2 * seg :], down_score + score
    last, last_score = unpack(send(pack(up, up_score), TO_UP))
    total, total_score = last + down, last_score + down_score
    side, side_score = unpack(send(pack(total[:, seg:], total_score), TO_SIDE))
    own, own_score = total[:, :seg] + side, total_score + side_score
    other_score = send(total_score, TO_CORE) + send(total_score, TO_CROSS)

    row_scores = jnp.concatenate([own_score, other_score], axis=1).reshape(2 * rows, 1)
    slopes = jnp.concatenate([slopes_mine, slopes_other], axis=0)
    both = jnp.concatenate([mine_rows, other_rows], axis=0)
    core_cols = width // 2
    router_part = dot(
        jnp.concatenate(split3(slopes * row_scores), axis=1),
        columns(both, width + core * core_cols, core_cols),
        ((0,), (0,)),
    )
    router_part = (router_part[:experts] + router_part[experts : 2 * experts]) + router_part[
        2 * experts :
    ]

    score_high = lax.reduce_precision(own_score, 8, 7)
    score_rows = jnp.concatenate([score_high, own_score - score_high], axis=0)
    score_rows = jnp.transpose(score_rows.reshape(2, experts, half), (1, 0, 2))
    score_rows = jnp.pad(score_rows, ((0, 0), (0, 6), (0, seg - half))).astype(BF16)
    router_rows = router_part.astype(BF16).reshape(-1, seg)
    home = lax.all_to_all(
        jnp.concatenate(
            [
                own.astype(BF16).reshape(experts, half, seg),
                score_rows,
                jnp.broadcast_to(router_rows[None], (EP,) + router_rows.shape),
            ],
            axis=1,
        ),
        "ep",
        0,
        0,
        tiled=True,
    )
    returned = home[:, :half].reshape(rows, seg)
    back_scores = jnp.sum(home[:, half : half + 8, :half].astype(F32), axis=1)
    router_mine = jnp.sum(home[:, half + 8 :].astype(F32), axis=0) / (tok_rows * EP)
    router_mine = router_mine.reshape(experts, core_cols)
    merged = dot(spread_abs, returned, ((1,), (0,)))
    taken = jnp.sum(
        jnp.where(places_abs, back_scores.reshape(1, 1, rows), 0.0), axis=2
    )
    low_cols, high_cols = merged[:, :own_cols], merged[:, own_cols:]
    keep = jnp.where(core == 0, low_cols, high_cols)
    give = jnp.where(core == 0, high_cols, low_cols)
    expert_grad = keep + send(give.astype(BF16), TO_CORE).astype(F32)
    small = jnp.concatenate([router_mine, jnp.pad(taken.T, ((0, 6), (0, 0)))], axis=1)
    got_small = send(small, TO_CORE)
    taken = (taken.T + got_small[:2, core_cols:]).T
    router_other = got_small[:, :core_cols]
    grad_router = jnp.concatenate(
        [
            jnp.where(core == 0, router_mine, router_other),
            jnp.where(core == 0, router_other, router_mine),
        ],
        axis=1,
    )
    change = first_gate * second_gate * (taken[:, 0] - taken[:, 1])
    logit_grad = change[:, None] * (chosen_hot[:, 0, :] - chosen_hot[:, 1, :])

    weighted = jnp.concatenate([weighted_mine, weighted_other], axis=0)
    act_grad = jnp.concatenate([act_mine, act_other], axis=0)
    grad_out = dot(weighted, both[:, :width], ((0,), (0,))).astype(BF16)
    grad_in = dot(act_grad, both[:, width : 2 * width], ((0,), (0,))).astype(BF16)

    router_rows = lax.dynamic_slice_in_dim(router_weight, fsdp_index * own_cols, own_cols, 0)
    grad_tokens = (
        expert_grad + jnp.dot(logit_grad, router_rows.T, precision=lax.Precision.HIGHEST)
    ).astype(BF16)
    return grad_tokens, grad_in.T[None], grad_out[None], grad_router.T


def solution(mesh):
    placed = (
        P("ep", None),
        P("ep", None),
        P(),
        P("ep", None, "fsdp"),
        P("ep", "fsdp", None),
        P("ep", None),
        P("ep", None),
    )
    return jax.shard_map(
        per_device,
        mesh=mesh,
        in_specs=placed,
        out_specs=(P("ep", "fsdp"), P("ep", None, "fsdp"), P("ep", "fsdp", None), P()),
        check_vma=False,
    )
```

```python
import jax
import jax.numpy as jnp
from jax import lax
from jax.sharding import PartitionSpec as P

F32 = jnp.float32
BF16 = jnp.bfloat16
Z = 8
EP = 8


def fsdp_pairs(move):
    pairs = []
    for lo in range(2):
        for z in range(Z):
            for core in range(2):
                a, b, c = move(lo, z, core)
                pairs.append(((lo * Z + z) * 2 + core, ((a % 2) * Z + b % Z) * 2 + c % 2))
    return pairs


TO_CORE = fsdp_pairs(lambda lo, z, core: (lo, z, core + 1))
TO_UP = fsdp_pairs(lambda lo, z, core: (lo, z + 1, core))
TO_DOWN = fsdp_pairs(lambda lo, z, core: (lo, z - 1, core))
TO_SIDE = fsdp_pairs(lambda lo, z, core: (lo + 1, z, core))

TO_CROSS = fsdp_pairs(lambda lo, z, core: (lo + 1, z, core + 1))


def send(array, pairs):
    return lax.ppermute(array, "fsdp", pairs)


def dot(left, right, dims):
    return lax.dot_general(left, right, (dims, ((), ())), preferred_element_type=F32)


def split3(array):
    high = lax.reduce_precision(array, 8, 7)
    rest = array - high
    mid = lax.reduce_precision(rest, 8, 7)
    low = rest - mid
    return high.astype(BF16), mid.astype(BF16), low.astype(BF16)


def columns(array, start, size):
    return lax.dynamic_slice_in_dim(array, start, size, 1)


def per_device(tokens, out_grad, router_weight, expert_in, expert_out, choices, slots):
    tok_rows, width = tokens.shape
    experts = router_weight.shape[1]
    capacity = max(2, 2 * tok_rows // experts)
    half = capacity // 2
    rows = experts * half
    fsdp_index = lax.axis_index("fsdp")
    me = lax.axis_index("ep")
    core = fsdp_index % 2
    z = (fsdp_index // 2) % Z
    lo = fsdp_index // (2 * Z)
    seg = width // (2 * Z)
    core_cols = width // 2
    own_cols = width // (4 * Z)

    w_in = expert_in[0].T
    w_out = expert_out[0]
    hidden_own = w_in.shape[0]
    w_in = jnp.concatenate([w_in, send(w_in, TO_CORE)], axis=0)
    w_out = jnp.concatenate([w_out, send(w_out, TO_CORE)], axis=0)

    key_abs = jnp.where((slots // half == core) & (slots >= 0), choices * half + slots % half, -1)
    places_abs = key_abs[:, :, None] == jnp.arange(rows, dtype=jnp.int32)
    spread_abs = (places_abs[:, 0] | places_abs[:, 1]).astype(BF16)
    both_choices = jnp.broadcast_to(
        jnp.sum(choices, axis=1, keepdims=True).astype(BF16), (tok_rows, 128)
    )
    packed = jnp.concatenate([out_grad, tokens, both_choices], axis=1)
    send_rows = dot(spread_abs, packed, ((0,), (0,))).astype(BF16)
    send_rows, router_weight = lax.optimization_barrier((send_rows, router_weight))
    mine_rows = lax.all_to_all(
        send_rows.reshape(experts, half, 2 * width + 128), "ep", 0, 0, tiled=True
    ).reshape(rows, 2 * width + 128)
    router_parts = jnp.concatenate(split3(router_weight), axis=1)
    logits = dot(tokens, router_parts, ((1,), (0,)))
    logits = (logits[:, :experts] + logits[:, experts : 2 * experts]) + logits[:, 2 * experts :]
    chosen_hot = (choices[:, :, None] == jnp.arange(experts, dtype=jnp.int32)).astype(F32)
    chosen = jnp.sum(chosen_hot * logits[:, None, :], axis=2)
    first_gate = 1.0 / (1.0 + jnp.exp(chosen[:, 1] - chosen[:, 0]))
    second_gate = 1.0 / (1.0 + jnp.exp(chosen[:, 0] - chosen[:, 1]))

    w_ext = jnp.concatenate([w_in, router_parts.T], axis=0)

    def weights(k):
        at = (z + k) % Z
        return [columns(w_in, ((lo ^ d) * Z + at) * seg, seg) for d in range(2)]

    orders = [(4, 5), (3, 6), (2, 7), (1, 0)]
    near = [jnp.concatenate(weights(a) + weights(b), axis=1) for a, b in orders]

    mine_rows, w_ext, w_out, near = lax.optimization_barrier((mine_rows, w_ext, w_out, near))
    hidden_count = w_in.shape[0]

    def act(part_rows):
        ext = dot(part_rows[:, width : 2 * width], w_ext, ((1,), (1,)))
        back = dot(part_rows[:, :width], w_out, ((1,), (1,)))
        pre = ext[:, :hidden_count]
        row_logits = ext[:, hidden_count : hidden_count + experts] + (
            ext[:, hidden_count + experts : hidden_count + 2 * experts]
            + ext[:, hidden_count + 2 * experts :]
        )
        second = part_rows[:, 2 * width : 2 * width + 1].astype(jnp.int32) - me
        ids = jnp.arange(experts, dtype=jnp.int32)[None, :]
        gap = jnp.sum(
            jnp.where(ids == second, row_logits, 0.0) - jnp.where(ids == me, row_logits, 0.0),
            axis=1,
            keepdims=True,
        )
        gate_wide = 1.0 / (1.0 + jnp.exp(gap))
        slope = gate_wide * (1.0 / (1.0 + jnp.exp(-gap)))
        gate = gate_wide.astype(BF16).astype(F32)
        sig = jax.nn.sigmoid(pre)
        hidden = (pre * sig).astype(BF16)
        hid_wide = hidden.astype(F32)
        score = jnp.sum(hid_wide * back, axis=1)[None]
        weighted = (hid_wide * gate).astype(BF16)
        act_grad = (gate * back * sig * (1.0 + pre * (1.0 - sig))).astype(BF16)
        slopes = slope * ((ids == me).astype(F32) - (ids == second).astype(F32))
        return score, weighted, act_grad, slopes

    score, weighted, act_grad, slopes = act(mine_rows)

    def pack(grads, score):
        high = lax.reduce_precision(score, 8, 7)
        block = jnp.concatenate([high, score - high], axis=0)
        block = jnp.pad(block, ((0, 6), (0, grads.shape[1] - rows)))
        return jnp.concatenate([grads, block], axis=0).astype(BF16)

    def unpack(packed):
        wide = packed.astype(F32)
        return wide[:rows], jnp.sum(wide[rows:, :rows], axis=0, keepdims=True)

    part = dot(act_grad, near[0], ((1,), (0,)))
    up, down = part[:, : 2 * seg], part[:, 2 * seg :]
    up_score = down_score = score
    later = (act_grad, weighted, slopes, mine_rows)
    grads = ()
    for step in range(3):
        going_up, going_down, later, grads = lax.optimization_barrier(
            (pack(up, up_score), pack(down, down_score), later, grads)
        )
        up, up_score = unpack(send(going_up, TO_UP))
        down, down_score = unpack(send(going_down, TO_DOWN))
        act_grad, weighted, slopes, mine_rows = later
        part = dot(act_grad, near[step + 1], ((1,), (0,)))
        up, up_score = up + part[:, : 2 * seg], up_score + score
        down, down_score = down + part[:, 2 * seg :], down_score + score
        if step == 0:
            other_rows = send(mine_rows, TO_CORE)
            other_acts = send(
                jnp.concatenate([act_grad[:, hidden_own:], weighted[:, hidden_own:]], axis=1),
                TO_CORE,
            )
            grads = (other_rows, other_acts, send(slopes, TO_CORE))
        elif step == 1:
            other_rows, other_acts, other_slopes = grads
            both = jnp.concatenate([mine_rows, other_rows], axis=0)
            act_all = jnp.concatenate([act_grad[:, :hidden_own], other_acts[:, :hidden_own]])
            weighted_all = jnp.concatenate([weighted[:, :hidden_own], other_acts[:, hidden_own:]])
            half_x = columns(both, width + core * core_cols, core_cols)
            grads = (both, act_all, weighted_all, jnp.concatenate([slopes, other_slopes]), half_x)
        else:
            grad_out = dot(grads[2], grads[0][:, :width], ((0,), (0,))).astype(BF16)
    both, act_all, _, slopes, half_x = grads
    up, up_score, act_all, grad_out = lax.optimization_barrier((up, up_score, act_all, grad_out))
    grad_in = dot(act_all, both[:, width : 2 * width], ((0,), (0,))).astype(BF16)
    last, last_score = unpack(send(pack(up, up_score), TO_UP))
    total, total_score = last + down, last_score + down_score
    side, side_score = unpack(send(pack(total[:, seg:], total_score), TO_SIDE))
    own, own_score = total[:, :seg] + side, total_score + side_score
    other_score = send(total_score, TO_CORE) + send(total_score, TO_CROSS)

    row_scores = jnp.concatenate([own_score, other_score], axis=1).reshape(2 * rows, 1)
    router_part = dot(
        jnp.concatenate(split3(slopes * row_scores), axis=1),
        half_x,
        ((0,), (0,)),
    )
    router_part = (router_part[:experts] + router_part[experts : 2 * experts]) + router_part[
        2 * experts :
    ]

    score_high = lax.reduce_precision(own_score, 8, 7)
    score_rows = jnp.concatenate([score_high, own_score - score_high], axis=0)
    score_rows = jnp.transpose(score_rows.reshape(2, experts, half), (1, 0, 2))
    score_rows = jnp.pad(score_rows, ((0, 0), (0, 6), (0, seg - half))).astype(BF16)
    router_rows = router_part.astype(BF16).reshape(-1, seg)
    home = lax.all_to_all(
        jnp.concatenate(
            [
                own.astype(BF16).reshape(experts, half, seg),
                score_rows,
                jnp.broadcast_to(router_rows[None], (EP,) + router_rows.shape),
            ],
            axis=1,
        ),
        "ep",
        0,
        0,
        tiled=True,
    )
    returned = home[:, :half].reshape(rows, seg)
    back_scores = jnp.sum(home[:, half : half + 8, :half].astype(F32), axis=1)
    router_mine = jnp.sum(home[:, half + 8 :].astype(F32), axis=0) / (tok_rows * EP)
    router_mine = router_mine.reshape(experts, core_cols)
    merged = dot(spread_abs, returned, ((1,), (0,)))
    taken = jnp.sum(
        jnp.where(places_abs, back_scores.reshape(1, 1, rows), 0.0), axis=2
    )
    low_cols, high_cols = merged[:, :own_cols], merged[:, own_cols:]
    keep = jnp.where(core == 0, low_cols, high_cols)
    give = jnp.where(core == 0, high_cols, low_cols)
    expert_grad = keep + send(give.astype(BF16), TO_CORE).astype(F32)
    small = jnp.concatenate([router_mine, jnp.pad(taken.T, ((0, 6), (0, 0)))], axis=1)
    got_small = send(small, TO_CORE)
    taken = (taken.T + got_small[:2, core_cols:]).T
    router_other = got_small[:, :core_cols]
    grad_router = jnp.concatenate(
        [
            jnp.where(core == 0, router_mine, router_other),
            jnp.where(core == 0, router_other, router_mine),
        ],
        axis=1,
    )
    change = first_gate * second_gate * (taken[:, 0] - taken[:, 1])
    logit_grad = change[:, None] * (chosen_hot[:, 0, :] - chosen_hot[:, 1, :])

    router_rows = lax.dynamic_slice_in_dim(router_weight, fsdp_index * own_cols, own_cols, 0)
    grad_tokens = (
        expert_grad + jnp.dot(logit_grad, router_rows.T, precision=lax.Precision.HIGHEST)
    ).astype(BF16)
    return grad_tokens, grad_in.T[None], grad_out[None], grad_router.T


def solution(mesh):
    placed = (
        P("ep", None),
        P("ep", None),
        P(),
        P("ep", None, "fsdp"),
        P("ep", "fsdp", None),
        P("ep", None),
        P("ep", None),
    )
    return jax.shard_map(
        per_device,
        mesh=mesh,
        in_specs=placed,
        out_specs=(P("ep", "fsdp"), P("ep", None, "fsdp"), P("ep", "fsdp", None), P()),
        check_vma=False,
    )
```

```python
import jax
import jax.numpy as jnp
from jax import lax
from jax.sharding import PartitionSpec as P

F32 = jnp.float32
BF16 = jnp.bfloat16
Z = 8
EP = 8


def fsdp_pairs(move):
    pairs = []
    for lo in range(2):
        for z in range(Z):
            for core in range(2):
                a, b, c = move(lo, z, core)
                pairs.append(((lo * Z + z) * 2 + core, ((a % 2) * Z + b % Z) * 2 + c % 2))
    return pairs


TO_CORE = fsdp_pairs(lambda lo, z, core: (lo, z, core + 1))
TO_UP = fsdp_pairs(lambda lo, z, core: (lo, z + 1, core))
TO_DOWN = fsdp_pairs(lambda lo, z, core: (lo, z - 1, core))
TO_SIDE = fsdp_pairs(lambda lo, z, core: (lo + 1, z, core))

TO_CROSS = fsdp_pairs(lambda lo, z, core: (lo + 1, z, core + 1))


def send(array, pairs):
    return lax.ppermute(array, "fsdp", pairs)


def dot(left, right, dims):
    return lax.dot_general(left, right, (dims, ((), ())), preferred_element_type=F32)


def split3(array):
    high = lax.reduce_precision(array, 8, 7)
    rest = array - high
    mid = lax.reduce_precision(rest, 8, 7)
    low = rest - mid
    return high.astype(BF16), mid.astype(BF16), low.astype(BF16)


def columns(array, start, size):
    return lax.dynamic_slice_in_dim(array, start, size, 1)


def per_device(tokens, out_grad, router_weight, expert_in, expert_out, choices, slots):
    tok_rows, width = tokens.shape
    experts = router_weight.shape[1]
    capacity = max(2, 2 * tok_rows // experts)
    half = capacity // 2
    rows = experts * half
    fsdp_index = lax.axis_index("fsdp")
    me = lax.axis_index("ep")
    core = fsdp_index % 2
    z = (fsdp_index // 2) % Z
    lo = fsdp_index // (2 * Z)
    seg = width // (2 * Z)
    core_cols = width // 2
    own_cols = width // (4 * Z)

    w_in = expert_in[0].T
    w_out = expert_out[0]
    hidden_own = w_in.shape[0]
    w_in = jnp.concatenate([w_in, send(w_in, TO_CORE)], axis=0)
    w_out = jnp.concatenate([w_out, send(w_out, TO_CORE)], axis=0)

    key_abs = jnp.where((slots // half == core) & (slots >= 0), choices * half + slots % half, -1)
    places_abs = key_abs[:, :, None] == jnp.arange(rows, dtype=jnp.int32)
    spread_abs = (places_abs[:, 0] | places_abs[:, 1]).astype(BF16)
    both_choices = jnp.broadcast_to(
        jnp.sum(choices, axis=1, keepdims=True).astype(BF16), (tok_rows, 128)
    )
    packed = jnp.concatenate([out_grad, tokens, both_choices], axis=1)
    send_rows = dot(spread_abs, packed, ((0,), (0,))).astype(BF16)
    send_rows, router_weight = lax.optimization_barrier((send_rows, router_weight))
    mine_rows = lax.all_to_all(
        send_rows.reshape(experts, half, 2 * width + 128), "ep", 0, 0, tiled=True
    ).reshape(rows, 2 * width + 128)
    router_parts = jnp.concatenate(split3(router_weight), axis=1)
    logits = dot(tokens, router_parts, ((1,), (0,)))
    logits = (logits[:, :experts] + logits[:, experts : 2 * experts]) + logits[:, 2 * experts :]
    chosen_hot = (choices[:, :, None] == jnp.arange(experts, dtype=jnp.int32)).astype(F32)
    chosen = jnp.sum(chosen_hot * logits[:, None, :], axis=2)
    first_gate = 1.0 / (1.0 + jnp.exp(chosen[:, 1] - chosen[:, 0]))
    second_gate = 1.0 / (1.0 + jnp.exp(chosen[:, 0] - chosen[:, 1]))

    w_ext = jnp.concatenate([w_in, router_parts.T], axis=0)
    id_row = jnp.where(jnp.arange(width + 128)[None] == width, 1.0, 0.0).astype(BF16)
    w_ext = jnp.concatenate([jnp.pad(w_ext, ((0, 0), (0, 128))), id_row], axis=0)

    def weights(k):
        at = (z + k) % Z
        return [columns(w_in, ((lo ^ d) * Z + at) * seg, seg) for d in range(2)]

    orders = [(4, 5), (3, 6), (2, 7), (1, 0)]
    near = [jnp.concatenate(weights(a) + weights(b), axis=1) for a, b in orders]

    mine_rows, w_ext, w_out, near = lax.optimization_barrier((mine_rows, w_ext, w_out, near))
    hidden_count = w_in.shape[0]

    def act(part_rows):
        ext = dot(part_rows[:, width:], w_ext, ((1,), (1,)))
        back = dot(part_rows[:, :width], w_out, ((1,), (1,)))
        pre = ext[:, :hidden_count]
        row_logits = ext[:, hidden_count : hidden_count + experts] + (
            ext[:, hidden_count + experts : hidden_count + 2 * experts]
            + ext[:, hidden_count + 2 * experts : hidden_count + 3 * experts]
        )
        second = ext[:, hidden_count + 3 * experts :].astype(jnp.int32) - me
        ids = jnp.arange(experts, dtype=jnp.int32)[None, :]
        gap = jnp.sum(
            jnp.where(ids == second, row_logits, 0.0) - jnp.where(ids == me, row_logits, 0.0),
            axis=1,
            keepdims=True,
        )
        gate_wide = 1.0 / (1.0 + jnp.exp(gap))
        slope = gate_wide * (1.0 / (1.0 + jnp.exp(-gap)))
        gate = gate_wide.astype(BF16).astype(F32)
        sig = jax.nn.sigmoid(pre)
        hidden = (pre * sig).astype(BF16)
        hid_wide = hidden.astype(F32)
        score = jnp.sum(hid_wide * back, axis=1)[None]
        weighted = (hid_wide * gate).astype(BF16)
        act_grad = (gate * back * sig * (1.0 + pre * (1.0 - sig))).astype(BF16)
        slopes = slope * ((ids == me).astype(F32) - (ids == second).astype(F32))
        return score, weighted, act_grad, slopes

    score, weighted, act_grad, slopes = act(mine_rows)

    def pack(grads, score):
        high = lax.reduce_precision(score, 8, 7)
        block = jnp.concatenate([high, score - high], axis=0)
        block = jnp.pad(block, ((0, 6), (0, grads.shape[1] - rows)))
        return jnp.concatenate([grads, block], axis=0).astype(BF16)

    def unpack(packed):
        wide = packed.astype(F32)
        return wide[:rows], jnp.sum(wide[rows:, :rows], axis=0, keepdims=True)

    part = dot(act_grad, near[0], ((1,), (0,)))
    up, down = part[:, : 2 * seg], part[:, 2 * seg :]
    up_score = down_score = score
    later = (act_grad, weighted, slopes, mine_rows)
    grads = ()
    for step in range(3):
        going_up, going_down, later, grads = lax.optimization_barrier(
            (pack(up, up_score), pack(down, down_score), later, grads)
        )
        up, up_score = unpack(send(going_up, TO_UP))
        down, down_score = unpack(send(going_down, TO_DOWN))
        act_grad, weighted, slopes, mine_rows = later
        part = dot(act_grad, near[step + 1], ((1,), (0,)))
        up, up_score = up + part[:, : 2 * seg], up_score + score
        down, down_score = down + part[:, 2 * seg :], down_score + score
        if step == 0:
            other_rows = send(mine_rows, TO_CORE)
            other_acts = send(
                jnp.concatenate([act_grad[:, hidden_own:], weighted[:, hidden_own:]], axis=1),
                TO_CORE,
            )
            grads = (other_rows, other_acts, send(slopes, TO_CORE))
        elif step == 1:
            other_rows, other_acts, other_slopes = grads
            both = jnp.concatenate([mine_rows, other_rows], axis=0)
            act_all = jnp.concatenate([act_grad[:, :hidden_own], other_acts[:, :hidden_own]])
            weighted_all = jnp.concatenate([weighted[:, :hidden_own], other_acts[:, hidden_own:]])
            half_x = columns(both, width + core * core_cols, core_cols)
            grads = (both, act_all, weighted_all, jnp.concatenate([slopes, other_slopes]), half_x)
        else:
            grad_out = dot(grads[2], grads[0][:, :width], ((0,), (0,))).astype(BF16)
    both, act_all, _, slopes, half_x = grads
    up, up_score, act_all, grad_out = lax.optimization_barrier((up, up_score, act_all, grad_out))
    grad_in = dot(act_all, both[:, width : 2 * width], ((0,), (0,))).astype(BF16)
    last, last_score = unpack(send(pack(up, up_score), TO_UP))
    total, total_score = last + down, last_score + down_score
    side, side_score = unpack(send(pack(total[:, seg:], total_score), TO_SIDE))
    own, own_score = total[:, :seg] + side, total_score + side_score
    other_score = send(total_score, TO_CORE) + send(total_score, TO_CROSS)

    row_scores = jnp.concatenate([own_score, other_score], axis=1).reshape(2 * rows, 1)
    router_part = dot(
        jnp.concatenate(split3(slopes * row_scores), axis=1),
        half_x,
        ((0,), (0,)),
    )
    router_part = (router_part[:experts] + router_part[experts : 2 * experts]) + router_part[
        2 * experts :
    ]

    score_high = lax.reduce_precision(own_score, 8, 7)
    score_rows = jnp.concatenate([score_high, own_score - score_high], axis=0)
    score_rows = jnp.transpose(score_rows.reshape(2, experts, half), (1, 0, 2))
    score_rows = jnp.pad(score_rows, ((0, 0), (0, 6), (0, seg - half))).astype(BF16)
    router_rows = router_part.astype(BF16).reshape(-1, seg)
    home = lax.all_to_all(
        jnp.concatenate(
            [
                own.astype(BF16).reshape(experts, half, seg),
                score_rows,
                jnp.broadcast_to(router_rows[None], (EP,) + router_rows.shape),
            ],
            axis=1,
        ),
        "ep",
        0,
        0,
        tiled=True,
    )
    returned = home[:, :half].reshape(rows, seg)
    back_scores = jnp.sum(home[:, half : half + 8, :half].astype(F32), axis=1)
    router_mine = jnp.sum(home[:, half + 8 :].astype(F32), axis=0) / (tok_rows * EP)
    router_mine = router_mine.reshape(experts, core_cols)
    merged = dot(returned, spread_abs, ((0,), (1,)))
    taken = jnp.sum(
        jnp.where(places_abs, back_scores.reshape(1, 1, rows), 0.0), axis=2
    )
    low_cols, high_cols = merged[:own_cols], merged[own_cols:]
    keep = jnp.where(core == 0, low_cols, high_cols)
    give = jnp.where(core == 0, high_cols, low_cols)
    expert_grad = keep + send(give.astype(BF16), TO_CORE).astype(F32)
    small = jnp.concatenate([router_mine, jnp.pad(taken.T, ((0, 6), (0, 0)))], axis=1)
    got_small = send(small, TO_CORE)
    taken = (taken.T + got_small[:2, core_cols:]).T
    router_other = got_small[:, :core_cols]
    grad_router = jnp.concatenate(
        [
            jnp.where(core == 0, router_mine, router_other),
            jnp.where(core == 0, router_other, router_mine),
        ],
        axis=1,
    )
    change = first_gate * second_gate * (taken[:, 0] - taken[:, 1])
    logit_grad = change[:, None] * (chosen_hot[:, 0, :] - chosen_hot[:, 1, :])

    router_rows = lax.dynamic_slice_in_dim(router_weight, fsdp_index * own_cols, own_cols, 0)
    grad_tokens = (
        expert_grad
        + sum(router_rows[:, e : e + 1] * logit_grad.T[e : e + 1] for e in range(experts))
    ).astype(BF16)
    return grad_tokens.T, grad_in.T[None], grad_out[None], grad_router.T


def solution(mesh):
    placed = (
        P("ep", None),
        P("ep", None),
        P(),
        P("ep", None, "fsdp"),
        P("ep", "fsdp", None),
        P("ep", None),
        P("ep", None),
    )
    return jax.shard_map(
        per_device,
        mesh=mesh,
        in_specs=placed,
        out_specs=(P("ep", "fsdp"), P("ep", None, "fsdp"), P("ep", "fsdp", None), P()),
        check_vma=False,
    )
```

```python
import jax
import jax.numpy as jnp
from jax import lax
from jax.sharding import PartitionSpec as P

F32 = jnp.float32
BF16 = jnp.bfloat16
Z = 8
EP = 8


def fsdp_pairs(move):
    pairs = []
    for lo in range(2):
        for z in range(Z):
            for core in range(2):
                a, b, c = move(lo, z, core)
                pairs.append(((lo * Z + z) * 2 + core, ((a % 2) * Z + b % Z) * 2 + c % 2))
    return pairs


TO_CORE = fsdp_pairs(lambda lo, z, core: (lo, z, core + 1))
TO_UP = fsdp_pairs(lambda lo, z, core: (lo, z + 1, core))
TO_DOWN = fsdp_pairs(lambda lo, z, core: (lo, z - 1, core))
TO_SIDE = fsdp_pairs(lambda lo, z, core: (lo + 1, z, core))

TO_CROSS = fsdp_pairs(lambda lo, z, core: (lo + 1, z, core + 1))


def send(array, pairs):
    return lax.ppermute(array, "fsdp", pairs)


def dot(left, right, dims):
    return lax.dot_general(left, right, (dims, ((), ())), preferred_element_type=F32)


def split3(array):
    high = lax.reduce_precision(array, 8, 7)
    rest = array - high
    mid = lax.reduce_precision(rest, 8, 7)
    low = rest - mid
    return high.astype(BF16), mid.astype(BF16), low.astype(BF16)


def columns(array, start, size):
    return lax.dynamic_slice_in_dim(array, start, size, 1)


def per_device(tokens, out_grad, router_weight, expert_in, expert_out, choices, slots):
    tok_rows, width = tokens.shape
    experts = router_weight.shape[1]
    capacity = max(2, 2 * tok_rows // experts)
    half = capacity // 2
    rows = experts * half
    fsdp_index = lax.axis_index("fsdp")
    me = lax.axis_index("ep")
    core = fsdp_index % 2
    z = (fsdp_index // 2) % Z
    lo = fsdp_index // (2 * Z)
    seg = width // (2 * Z)
    core_cols = width // 2
    own_cols = width // (4 * Z)

    w_in = expert_in[0].T
    w_out = expert_out[0]
    hidden_own = w_in.shape[0]
    w_in = jnp.concatenate([w_in, send(w_in, TO_CORE)], axis=0)
    w_out = jnp.concatenate([w_out, send(w_out, TO_CORE)], axis=0)

    key_abs = jnp.where((slots // half == core) & (slots >= 0), choices * half + slots % half, -1)
    places_abs = key_abs[:, :, None] == jnp.arange(rows, dtype=jnp.int32)
    spread_abs = (places_abs[:, 0] | places_abs[:, 1]).astype(BF16)
    both_choices = jnp.broadcast_to(
        jnp.sum(choices, axis=1, keepdims=True).astype(BF16), (tok_rows, 128)
    )
    packed = jnp.concatenate([out_grad, tokens, both_choices], axis=1)
    send_rows = dot(spread_abs, packed, ((0,), (0,))).astype(BF16)
    send_rows, router_weight = lax.optimization_barrier((send_rows, router_weight))
    mine_rows = lax.all_to_all(
        send_rows.reshape(experts, half, 2 * width + 128), "ep", 0, 0, tiled=True
    ).reshape(rows, 2 * width + 128)
    router_parts = jnp.concatenate(split3(router_weight), axis=1)
    logits = dot(tokens, router_parts, ((1,), (0,)))
    logits = (logits[:, :experts] + logits[:, experts : 2 * experts]) + logits[:, 2 * experts :]
    chosen_hot = (choices[:, :, None] == jnp.arange(experts, dtype=jnp.int32)).astype(F32)
    chosen = jnp.sum(chosen_hot * logits[:, None, :], axis=2)
    first_gate = 1.0 / (1.0 + jnp.exp(chosen[:, 1] - chosen[:, 0]))
    second_gate = 1.0 / (1.0 + jnp.exp(chosen[:, 0] - chosen[:, 1]))

    w_ext = jnp.concatenate([w_in, router_parts.T], axis=0)
    id_row = jnp.where(jnp.arange(width + 128)[None] == width, 1.0, 0.0).astype(BF16)
    w_ext = jnp.concatenate([jnp.pad(w_ext, ((0, 0), (0, 128))), id_row], axis=0)

    def weights(k):
        at = (z + k) % Z
        return [columns(w_in, ((lo ^ d) * Z + at) * seg, seg) for d in range(2)]

    orders = [(4, 5), (3, 6), (2, 7), (1, 0)]
    near = [jnp.concatenate(weights(a) + weights(b), axis=1) for a, b in orders]

    w_ext = (w_ext[:, :core_cols], w_ext[:, core_cols:])
    ready = (w_ext, w_out, near, first_gate, second_gate, chosen_hot)
    mine_rows, ready = lax.optimization_barrier((mine_rows, ready))
    w_ext, w_out, near, first_gate, second_gate, chosen_hot = ready
    hidden_count = w_in.shape[0]

    def act(part_rows):
        middle = width + core_cols
        ext = dot(part_rows[:, width:middle], w_ext[0], ((1,), (1,)))
        ext = ext + dot(part_rows[:, middle:], w_ext[1], ((1,), (1,)))
        back = dot(part_rows[:, :width], w_out, ((1,), (1,)))
        pre = ext[:, :hidden_count]
        row_logits = ext[:, hidden_count : hidden_count + experts] + (
            ext[:, hidden_count + experts : hidden_count + 2 * experts]
            + ext[:, hidden_count + 2 * experts : hidden_count + 3 * experts]
        )
        second = ext[:, hidden_count + 3 * experts :].astype(jnp.int32) - me
        ids = jnp.arange(experts, dtype=jnp.int32)[None, :]
        gap = jnp.sum(
            jnp.where(ids == second, row_logits, 0.0) - jnp.where(ids == me, row_logits, 0.0),
            axis=1,
            keepdims=True,
        )
        gate_wide = 1.0 / (1.0 + jnp.exp(gap))
        slope = gate_wide * (1.0 / (1.0 + jnp.exp(-gap)))
        gate = gate_wide.astype(BF16).astype(F32)
        sig = jax.nn.sigmoid(pre)
        hidden = (pre * sig).astype(BF16)
        hid_wide = hidden.astype(F32)
        score = jnp.sum(hid_wide * back, axis=1)[None]
        weighted = (hid_wide * gate).astype(BF16)
        act_grad = (gate * back * sig * (1.0 + pre * (1.0 - sig))).astype(BF16)
        slopes = slope * ((ids == me).astype(F32) - (ids == second).astype(F32))
        return score, weighted, act_grad, slopes

    score, weighted, act_grad, slopes = act(mine_rows)

    def pack(grads, score):
        high = lax.reduce_precision(score, 8, 7)
        block = jnp.concatenate([high, score - high], axis=0)
        block = jnp.pad(block, ((0, 6), (0, grads.shape[1] - rows)))
        return jnp.concatenate([grads, block], axis=0).astype(BF16)

    def unpack(packed):
        wide = packed.astype(F32)
        return wide[:rows], jnp.sum(wide[rows:, :rows], axis=0, keepdims=True)

    part = dot(act_grad, near[0], ((1,), (0,)))
    up, down = part[:, : 2 * seg], part[:, 2 * seg :]
    up_score = down_score = score
    later = (act_grad, weighted, slopes, mine_rows)
    grads = ()
    for step in range(3):
        going_up, going_down, later, grads = lax.optimization_barrier(
            (pack(up, up_score), pack(down, down_score), later, grads)
        )
        up, up_score = unpack(send(going_up, TO_UP))
        down, down_score = unpack(send(going_down, TO_DOWN))
        act_grad, weighted, slopes, mine_rows = later
        part = dot(act_grad, near[step + 1], ((1,), (0,)))
        up, up_score = up + part[:, : 2 * seg], up_score + score
        down, down_score = down + part[:, 2 * seg :], down_score + score
        if step == 0:
            other_rows = send(mine_rows, TO_CORE)
            other_acts = send(
                jnp.concatenate([act_grad[:, hidden_own:], weighted[:, hidden_own:]], axis=1),
                TO_CORE,
            )
            grads = (other_rows, other_acts, send(slopes, TO_CORE))
        elif step == 1:
            other_rows, other_acts, other_slopes = grads
            both = jnp.concatenate([mine_rows, other_rows], axis=0)
            act_all = jnp.concatenate([act_grad[:, :hidden_own], other_acts[:, :hidden_own]])
            weighted_all = jnp.concatenate([weighted[:, :hidden_own], other_acts[:, hidden_own:]])
            half_x = columns(both, width + core * core_cols, core_cols)
            grads = (both, act_all, weighted_all, jnp.concatenate([slopes, other_slopes]), half_x)
        else:
            grad_out = dot(grads[2], grads[0][:, :width], ((0,), (0,))).astype(BF16)
    both, act_all, _, slopes, half_x = grads
    up, up_score, act_all, grad_out = lax.optimization_barrier((up, up_score, act_all, grad_out))
    grad_in = dot(act_all, both[:, width : 2 * width], ((0,), (0,))).astype(BF16)
    last, last_score = unpack(send(pack(up, up_score), TO_UP))
    total, total_score = last + down, last_score + down_score
    side, side_score = unpack(send(pack(total[:, seg:], total_score), TO_SIDE))
    own, own_score = total[:, :seg] + side, total_score + side_score
    other_score = send(total_score, TO_CORE) + send(total_score, TO_CROSS)

    row_scores = jnp.concatenate([own_score, other_score], axis=1).reshape(2 * rows, 1)
    router_part = dot(
        jnp.concatenate(split3(slopes * row_scores), axis=1),
        half_x,
        ((0,), (0,)),
    )
    router_part = (router_part[:experts] + router_part[experts : 2 * experts]) + router_part[
        2 * experts :
    ]

    score_high = lax.reduce_precision(own_score, 8, 7)
    score_rows = jnp.concatenate([score_high, own_score - score_high], axis=0)
    score_rows = jnp.transpose(score_rows.reshape(2, experts, half), (1, 0, 2))
    score_rows = jnp.pad(score_rows, ((0, 0), (0, 6), (0, seg - half))).astype(BF16)
    router_rows = router_part.astype(BF16).reshape(-1, seg)
    home = lax.all_to_all(
        jnp.concatenate(
            [
                own.astype(BF16).reshape(experts, half, seg),
                score_rows,
                jnp.broadcast_to(router_rows[None], (EP,) + router_rows.shape),
            ],
            axis=1,
        ),
        "ep",
        0,
        0,
        tiled=True,
    )
    returned = home[:, :half].reshape(rows, seg)
    back_scores = jnp.sum(home[:, half : half + 8, :half].astype(F32), axis=1)
    router_mine = jnp.sum(home[:, half + 8 :].astype(F32), axis=0) / (tok_rows * EP)
    router_mine = router_mine.reshape(experts, core_cols)
    merged = dot(returned, spread_abs, ((0,), (1,)))
    taken = jnp.sum(
        jnp.where(places_abs, back_scores.reshape(1, 1, rows), 0.0), axis=2
    )
    low_cols, high_cols = merged[:own_cols], merged[own_cols:]
    keep = jnp.where(core == 0, low_cols, high_cols)
    give = jnp.where(core == 0, high_cols, low_cols)
    expert_grad = keep + send(give.astype(BF16), TO_CORE).astype(F32)
    small = jnp.concatenate([router_mine, jnp.pad(taken.T, ((0, 6), (0, 0)))], axis=1)
    got_small = send(small, TO_CORE)
    taken = (taken.T + got_small[:2, core_cols:]).T
    router_other = got_small[:, :core_cols]
    grad_router = jnp.concatenate(
        [
            jnp.where(core == 0, router_mine, router_other),
            jnp.where(core == 0, router_other, router_mine),
        ],
        axis=1,
    )
    change = first_gate * second_gate * (taken[:, 0] - taken[:, 1])
    logit_grad = change[:, None] * (chosen_hot[:, 0, :] - chosen_hot[:, 1, :])

    router_rows = lax.dynamic_slice_in_dim(router_weight, fsdp_index * own_cols, own_cols, 0)
    grad_tokens = (
        expert_grad
        + sum(router_rows[:, e : e + 1] * logit_grad.T[e : e + 1] for e in range(experts))
    ).astype(BF16)
    return grad_tokens.T, grad_in.T[None], grad_out[None], grad_router.T


def solution(mesh):
    placed = (
        P("ep", None),
        P("ep", None),
        P(),
        P("ep", None, "fsdp"),
        P("ep", "fsdp", None),
        P("ep", None),
        P("ep", None),
    )
    return jax.shard_map(
        per_device,
        mesh=mesh,
        in_specs=placed,
        out_specs=(P("ep", "fsdp"), P("ep", None, "fsdp"), P("ep", "fsdp", None), P()),
        check_vma=False,
    )
```
